32 devices in a mesh: groups: 2 (over y), blk: 4 (over z), chan: 2 (over x), pair: 2 (over core).
Axes of the slice: x: 2, y: 2, z: 4, core: 2. Of those that a mesh axis runs over, the one named last changes fastest.
Arguments:
- pair_act: bfloat16 [128, 64, 128], P(('groups', 'blk'), ('chan', 'pair')), parts along dimension 0, may hold values from -6 to 6
- pair_mask: int32 [128, 64], P(('groups', 'blk'), ('chan', 'pair')), parts along dimension 0, may hold values 0 or 1
- in_gain: float32 [128], replicated, may hold values from 0.25 to 1.75
- in_bias: float32 [128], replicated, may hold values from -1.5 to 1.5
- w_proj: bfloat16 [128, 512], replicated, may hold values from -0.5 to 0.5
- w_gate: bfloat16 [128, 128], replicated, may hold values from -0.5 to 0.5
- w_out: bfloat16 [128, 128], replicated, may hold values from -0.5 to 0.5
- out_gain: float32 [128], replicated, may hold values from 0.25 to 1.75
- out_bias: float32 [128], replicated, may hold values from -1.5 to 1.5
Outputs:
- update_cols: bfloat16 [128, 4, 16, 128], P('groups', ('chan', 'pair'), 'blk'), parts along dimension 0
The draws below stay inside these ranges and needn't reach their ends.
There are 2 independent parts, one for each index of `groups`. The reference program is written for one: setup_inputs(seed, part) draws one part's arguments, and reference() takes and returns one part's arrays. A program takes and returns all parts, laid end to end along the dimension named above; an argument that names none is the same for every part. Nothing has to cross between parts.
All inputs are finite; a program needn't handle non-finite values. No bound on the sum of `pair_mask` on one device may be relied on, other than what follows from the above.
Results may differ from the reference program's by a relative error of at most 0.0072.
Values may be sent and summed in bfloat16 or wider, within the bound.
A program may use at most 64 MiB of HBM per device.

```python
import jax
import jax.numpy as jnp
from jax import lax

PAIR_DIM = 128
HIDDEN_SIZE = 128
ROWS = 16
RESIDUES = 64
SLABS = 4
SLAB_COLS = 16
N_BLK = 4


def touch_ends(array, key, smallest, top_value):
    shape = array.shape
    place = [jax.random.randint(jax.random.fold_in(key, axis), (), 0, shape[axis]) for axis in range(len(shape))]
    array = array.at[tuple(place)].set(smallest)
    longest = shape.index(max(shape))
    place[longest] = (place[longest] + 1) % shape[longest]
    return array.at[tuple(place)].set(top_value)


def levels(stream_key, dims, cuts, low, high):
    level = 1.0
    for position, blocks in cuts:
        heights = jax.random.uniform(jax.random.fold_in(jax.random.fold_in(stream_key, 6), position), (blocks,), jnp.float32, low / len(cuts), high / len(cuts))
        level = level * jnp.repeat(jnp.exp(heights), dims[position] // blocks).reshape((-1,) + (1,) * (len(dims) - 1 - position))
    return level


def noise(rng, extent, width, reach, shards=(), kind=jnp.bfloat16):
    array = width * jax.random.normal(rng, extent, jnp.float32)
    if shards:
        array = array * levels(rng, extent, shards, -0.22, 0.18)
    return jnp.clip(array, -reach, reach).astype(kind)


def setup_inputs(seed: int = 0, part: int = 0) -> dict:
    streams_of = jax.random.split(jax.random.key(seed), 10)
    part_splits = jax.random.split(jax.random.fold_in(streams_of[9], part), 10)
    pair_act = noise(part_splits[0], (RESIDUES, RESIDUES, PAIR_DIM), 1.0, 6.0, ((0, 4), (1, 4)))
    pair_mask = touch_ends((jax.random.randint(part_splits[1], (RESIDUES, RESIDUES), 0, 4) < 3).astype(jnp.int32), jax.random.fold_in(part_splits[1], 1), 0, 1)
    in_gain = jnp.clip(1.0 + 0.15 * jax.random.normal(streams_of[2], (PAIR_DIM,), jnp.float32), 0.25, 1.75)
    in_bias = noise(streams_of[3], (PAIR_DIM,), 0.3, 1.5, (), jnp.float32)
    w_proj = noise(streams_of[4], (PAIR_DIM, 4 * HIDDEN_SIZE), PAIR_DIM ** -0.5, 0.5)
    w_gate = noise(streams_of[5], (PAIR_DIM, PAIR_DIM), PAIR_DIM ** -0.5, 0.5)
    w_out = noise(streams_of[6], (HIDDEN_SIZE, PAIR_DIM), HIDDEN_SIZE ** -0.5, 0.5)
    out_gain = jnp.clip(1.0 + 0.15 * jax.random.normal(streams_of[7], (HIDDEN_SIZE,), jnp.float32), 0.25, 1.75)
    out_bias = noise(streams_of[8], (HIDDEN_SIZE,), 0.3, 1.5, (), jnp.float32)
    return dict(pair_act=pair_act, pair_mask=pair_mask, in_gain=in_gain, in_bias=in_bias, w_proj=w_proj, w_gate=w_gate, w_out=w_out, out_gain=out_gain, out_bias=out_bias)


def norm_axis(values, gain, bias, axis):
    mean = lax.optimization_barrier(jnp.mean(values, axis=axis, keepdims=True))
    centred = values - mean
    var = lax.optimization_barrier(jnp.mean(centred * centred, axis=axis, keepdims=True))
    return centred * lax.rsqrt(var + 1e-05) * gain + bias

def reference(pair_act, pair_mask, in_gain, in_bias, w_proj, w_gate, w_out, out_gain, out_bias):
    weights = w_proj.reshape(PAIR_DIM, 4, HIDDEN_SIZE).astype(jnp.float32)
    gate_weights = w_gate.astype(jnp.float32)

    def prepare(block):
        rows_act, rows_mask = block
        normed = norm_axis(rows_act.astype(jnp.float32), in_gain, in_bias, -1).astype(jnp.bfloat16)
        proj = jnp.einsum('rkd,dgh->ghrk', normed.astype(jnp.float32), weights)
        mask_f = rows_mask.astype(jnp.float32)
        left = (jax.nn.sigmoid(proj[0]) * proj[1] * mask_f).astype(jnp.bfloat16)
        right = (jax.nn.sigmoid(proj[2]) * proj[3] * mask_f).astype(jnp.bfloat16)
        gate = jax.nn.sigmoid(jnp.einsum('rkd,de->rke', normed.astype(jnp.float32), gate_weights))
        return (left, right, gate)
    act_blocks = pair_act.reshape(N_BLK, ROWS, RESIDUES, PAIR_DIM)
    mask_blocks = pair_mask.reshape(N_BLK, ROWS, RESIDUES)
    left, right, gate = lax.map(prepare, (act_blocks, mask_blocks))
    left = jnp.transpose(left, (1, 0, 2, 3)).reshape(HIDDEN_SIZE, RESIDUES, RESIDUES)
    right = jnp.transpose(right, (1, 0, 2, 3)).reshape(HIDDEN_SIZE, RESIDUES, RESIDUES)
    gate = gate.reshape(RESIDUES, RESIDUES, PAIR_DIM)
    tri = jnp.einsum('cik,cjk->cij', left.astype(jnp.float32), right.astype(jnp.float32))
    tri_norm = norm_axis(tri, out_gain[:, None, None], out_bias[:, None, None], 0).astype(jnp.bfloat16)
    linear = jnp.einsum('hij,hd->ijd', tri_norm.astype(jnp.float32), w_out.astype(jnp.float32))
    update = (gate * linear).astype(jnp.bfloat16)
    return update.reshape(RESIDUES, SLABS, SLAB_COLS, PAIR_DIM)
```

```python
import functools

import jax
import jax.numpy as jnp
from jax import lax
from jax.experimental import pallas as pl
from jax.experimental.pallas import tpu as pltpu
from jax.sharding import PartitionSpec as P


def from_behind(value, axis, by):
    count = lax.axis_size(axis)
    return lax.ppermute(value, axis, [(i, (i + by) % count) for i in range(count)])


def norm_axis(values, gain, bias, axis):
    mean = jnp.mean(values, axis=axis, keepdims=True)
    centred = values - mean
    var = jnp.mean(centred * centred, axis=axis, keepdims=True)
    return centred * lax.rsqrt(var + 1e-05) * gain + bias


def on_device(pair_act, pair_mask, in_gain, in_bias, w_proj, w_gate, w_out, out_gain, out_bias):
    rows, cols, width = pair_act.shape
    hidden = w_out.shape[0]
    blocks = lax.axis_size("blk")
    chans = lax.axis_size("chan")
    halves = lax.axis_size("pair")
    normed = norm_axis(pair_act.astype(jnp.float32), in_gain, in_bias, -1).astype(jnp.bfloat16)
    weights = w_proj.reshape(width, 4, hidden)
    proj = jnp.einsum("rkd,dgh->ghrk", normed, weights, preferred_element_type=jnp.float32)
    mask_f = pair_mask.astype(jnp.float32)
    left = (jax.nn.sigmoid(proj[0]) * proj[1] * mask_f).astype(jnp.bfloat16)
    right = (jax.nn.sigmoid(proj[2]) * proj[3] * mask_f).astype(jnp.bfloat16)
    left, right = (
        lax.all_to_all(left, "chan", split_axis=0, concat_axis=2, tiled=True),
        lax.all_to_all(right, "chan", split_axis=0, concat_axis=2, tiled=True),
    )
    subset = left.shape[0]
    me_index = lax.axis_index("blk")
    total = rows * blocks
    zero_index = jnp.zeros((), jnp.int32)

    def place(acc, block, owner):
        part = jnp.einsum("cik,cjk->cij", left, block, preferred_element_type=jnp.float32)
        start = owner * rows
        return lax.dynamic_update_slice(acc, part, (zero_index, zero_index, start))

    acc = jnp.zeros((subset, rows, total), jnp.float32)
    acc = place(acc, right, me_index)

    def both_step(step, carry):
        acc_now, ahead, behind = carry
        ahead = from_behind(ahead, "blk", 1)
        behind = from_behind(behind, "blk", -1)
        acc_now = place(acc_now, ahead, (me_index - step) % blocks)
        acc_now = place(acc_now, behind, (me_index + step) % blocks)
        return (acc_now, ahead, behind)

    acc, ahead, behind = lax.fori_loop(1, (blocks - 1) // 2 + 1, both_step, (acc, right, right))
    ahead = from_behind(ahead, "blk", 1)
    acc = place(acc, ahead, (me_index - blocks // 2) % blocks)
    parts = acc.reshape(subset, rows, chans, halves, cols)
    mine = lax.psum_scatter(parts, "pair", scatter_dimension=3, tiled=True)
    full = lax.all_to_all(mine, "chan", split_axis=2, concat_axis=0, tiled=True)
    full = full.reshape(hidden, rows, cols)
    tri_norm = norm_axis(full, out_gain[:, None, None], out_bias[:, None, None], 0).astype(
        jnp.bfloat16
    )
    linear = jnp.einsum("hrj,hd->rjd", tri_norm, w_out, preferred_element_type=jnp.float32)
    gate = jax.nn.sigmoid(
        jnp.einsum("rjd,de->rje", normed, w_gate, preferred_element_type=jnp.float32)
    )
    update = (gate * linear).astype(jnp.bfloat16).reshape(rows, 1, cols, width)
    return lax.all_to_all(update, "blk", split_axis=2, concat_axis=0, tiled=True)


MESH = pl.DeviceIdType.MESH
CELLS = 16
GROUP = 8
PIECE = 4


def dot(a, b, contract):
    return lax.dot_general(a, b, ((contract[:1], contract[1:]), ((), ())), preferred_element_type=jnp.float32)


def kernel(
    blocks, chans, halves,
    act, mask, in_gain, in_bias, w_proj, w_gate, w_out, out_gain, out_bias,
    out,
    swap, normed, cells, pick, sides, sides_in, tri_f, tri, tri_in, squares, rows_out,
    side_send, side_recv, cell_send, cell_recv, tri_send, tri_recv,
):
    slabs = chans * halves
    blk = lax.axis_index("blk")
    slab = lax.axis_index("chan") * halves + lax.axis_index("pair")
    me = slab * blocks + blk
    others = [(ds, db) for db in range(blocks) for ds in range(slabs)]

    def peer(ds, db):
        s = (slab + ds) % slabs
        b = (blk + db) % blocks
        return s, b, s * blocks + b, {"blk": b, "chan": s // halves, "pair": s % halves}

    barrier = pltpu.get_barrier_semaphore()
    for ds, db in others[1:]:
        pl.semaphore_signal(barrier, inc=1, device_id=peer(ds, db)[3], device_id_type=MESH)

    x = act[...].astype(jnp.float32)
    mean = jnp.mean(x, axis=-1, keepdims=True)
    centred = x - mean
    var = jnp.mean(centred * centred, axis=-1, keepdims=True)
    x = centred * lax.rsqrt(var + 1e-05) * in_gain[...].reshape(1, 1, -1) + in_bias[...].reshape(1, 1, -1)
    for i in range(CELLS):
        swap[pl.ds(i, CELLS, stride=CELLS), :] = x[i]
    z = swap[...].astype(jnp.bfloat16)
    normed[...] = z.reshape(normed.shape)

    lanes = CELLS * CELLS
    row = lax.broadcasted_iota(jnp.int32, (CELLS, lanes), 0)
    lane = lax.broadcasted_iota(jnp.int32, (CELLS, lanes), 1)
    spread = jnp.where(lane // CELLS == row, 1.0, 0.0).astype(jnp.bfloat16)
    mask_rows = dot(mask[...].astype(jnp.float32).astype(jnp.bfloat16), spread, (1, 0))
    own_row = lane % CELLS == row
    mask_row = jnp.sum(jnp.where(own_row, mask_rows, 0.0), axis=0, keepdims=True)

    proj = dot(w_proj[...], z, (0, 1))
    hidden = proj.shape[0] // 4
    left = jax.nn.sigmoid(proj[:hidden]) * proj[hidden:2 * hidden] * mask_row
    right = jax.nn.sigmoid(proj[2 * hidden:3 * hidden]) * proj[3 * hidden:] * mask_row
    groups = hidden // GROUP
    both = jnp.concatenate(
        [left.reshape(groups, GROUP, lanes), right.reshape(groups, GROUP, lanes)], axis=1
    )
    sides[...] = both.astype(jnp.bfloat16)

    pl.semaphore_wait(barrier, len(others) - 1)
    copies = []
    for n, (ds, db) in list(enumerate(others))[:0:-1]:
        _, _, to, device = peer(ds, db)
        copy = pltpu.make_async_remote_copy(
            src_ref=sides.at[to], dst_ref=sides_in.at[me],
            send_sem=side_send.at[n], recv_sem=side_recv.at[me],
            device_id=device, device_id_type=MESH,
        )
        copy.start()
        copies.append(copy)
    for db in range(1, blocks):
        b = (blk + db) % blocks
        copy = pltpu.make_async_remote_copy(
            src_ref=normed.at[pl.ds(b * PIECE, PIECE)], dst_ref=cells.at[blk],
            send_sem=cell_send.at[db], recv_sem=cell_recv.at[blk],
            device_id={"blk": b}, device_id_type=MESH,
        )
        copy.start()
        copies.append(copy)
    sides_in[me] = sides[me]
    cells[blk] = normed[pl.ds(blk * PIECE, PIECE)]

    total = slabs * CELLS
    at = lax.broadcasted_iota(jnp.int32, (lanes, total), 0)
    col = lax.broadcasted_iota(jnp.int32, (lanes, total), 1)
    for s in range(slabs):
        pick[s] = jnp.where(col == at // CELLS + s * CELLS, 1.0, 0.0).astype(jnp.bfloat16)
    moved = (row % GROUP) // 2 * PIECE + row // GROUP * 2 + row % 2
    right_row = lane % CELLS == moved
    gain = jnp.transpose(jnp.broadcast_to(out_gain[...].reshape(1, -1), (hidden, hidden))).reshape(groups, GROUP, hidden)
    bias = jnp.transpose(jnp.broadcast_to(out_bias[...].reshape(1, -1), (hidden, hidden))).reshape(groups, GROUP, hidden)

    for db in range(blocks):
        acc = None
        for ds in range(slabs):
            s, b, frm, device = peer(ds, db)
            if (ds, db) != (0, 0):
                pltpu.make_async_remote_copy(
                    src_ref=sides.at[frm], dst_ref=sides_in.at[frm],
                    send_sem=side_send.at[0], recv_sem=side_recv.at[frm],
                    device_id=device, device_id_type=MESH,
                ).wait_recv()
            part = sides_in[frm].astype(jnp.float32)
            part_left = jnp.where(own_row[None], part[:GROUP][:, None, :], 0.0)
            part_right = jnp.where(right_row[None], part[GROUP:][:, None, :], 0.0)
            wide = jnp.concatenate([part_left, part_right], axis=0).reshape(2 * GROUP * CELLS, lanes)
            term = dot(wide.astype(jnp.bfloat16), pick[s], (1, 0))
            acc = term if acc is None else acc + term
        b = (blk + db) % blocks
        rows_of = pl.ds(pl.multiple_of(b * CELLS, CELLS), CELLS)
        block = acc.astype(jnp.bfloat16).reshape(2 * GROUP, CELLS, total)
        squares[:, rows_of, :] = block

    wide_rows = blocks * GROUP
    for h in range(GROUP):
        t = dot(squares[GROUP + h], squares[h], (1, 1)).reshape(blocks, 2, GROUP, total)
        t = jnp.concatenate([t[:, 0], t[:, 1]], axis=-1).reshape(wide_rows, 2 * total)
        tri_f[pl.ds(h, wide_rows, stride=GROUP), :] = t
    tri[...] = tri_f[...].astype(jnp.bfloat16).reshape(tri.shape)

    for n, (ds, db) in list(enumerate(others))[:0:-1]:
        _, _, to, device = peer(ds, db)
        copy = pltpu.make_async_remote_copy(
            src_ref=tri.at[to], dst_ref=tri_in.at[me],
            send_sem=tri_send.at[n], recv_sem=tri_recv.at[me],
            device_id=device, device_id_type=MESH,
        )
        copy.start()
        copies.append(copy)
    tri_in[me] = tri[me]

    for db in range(1, blocks):
        b = (blk + db) % blocks
        pltpu.make_async_remote_copy(
            src_ref=cells.at[b], dst_ref=cells.at[b],
            send_sem=cell_send.at[0], recv_sem=cell_recv.at[b],
            device_id={"blk": b}, device_id_type=MESH,
        ).wait_recv()
    mine = jnp.concatenate([cells[b, m] for m in range(PIECE) for b in range(blocks)], axis=0)
    gate = jax.nn.sigmoid(dot(mine, w_gate[...], (1, 0)))

    for ds, db in others[1:]:
        _, _, frm, device = peer(ds, db)
        pltpu.make_async_remote_copy(
            src_ref=tri.at[frm], dst_ref=tri_in.at[frm],
            send_sem=tri_send.at[0], recv_sem=tri_recv.at[frm],
            device_id=device, device_id_type=MESH,
        ).wait_recv()
    full = tri_in[...].astype(jnp.float32).reshape(groups, 2, GROUP, hidden)
    for q in range(2):
        t = full[:, q]
        mean = jnp.mean(t, axis=(0, 1), keepdims=True)
        centred = t - mean
        var = jnp.mean(centred * centred, axis=(0, 1), keepdims=True)
        t = centred * lax.rsqrt(var + 1e-05) * gain + bias
        linear = dot(t.reshape(hidden, hidden).astype(jnp.bfloat16), w_out[...], (0, 0))
        for p in range(2):
            m = p * 2 + q
            rows_out[pl.ds(m, total, stride=PIECE), :] = linear[p * total:(p + 1) * total] * gate[m * total:(m + 1) * total]
    out[...] = rows_out[...].astype(jnp.bfloat16)
    for copy in copies:
        copy.wait_send()


def in_one_kernel(*args):
    blocks = lax.axis_size("blk")
    chans = lax.axis_size("chan")
    halves = lax.axis_size("pair")
    rows, cols, width = args[0].shape
    slabs = chans * halves
    devices = blocks * slabs
    total = rows * blocks
    bf16, f32 = jnp.bfloat16, jnp.float32
    dma = pltpu.SemaphoreType.DMA
    vmem = pl.BlockSpec(memory_space=pltpu.VMEM)
    out = pl.pallas_call(
        functools.partial(kernel, blocks, chans, halves),
        out_shape=jax.ShapeDtypeStruct((total * PIECE, width), bf16),
        in_specs=[vmem] * len(args),
        out_specs=vmem,
        scratch_shapes=[
            pltpu.VMEM((rows * cols, width), f32),
            pltpu.VMEM((cols, rows, width), bf16),
            pltpu.VMEM((blocks, PIECE, rows, width), bf16),
            pltpu.VMEM((slabs, rows * cols, total), bf16),
            pltpu.VMEM((devices, 2 * GROUP, rows * cols), bf16),
            pltpu.VMEM((devices, 2 * GROUP, rows * cols), bf16),
            pltpu.VMEM((devices * 2 * GROUP, 2 * total), f32),
            pltpu.VMEM((devices, 2 * GROUP, 2 * total), bf16),
            pltpu.VMEM((devices, 2 * GROUP, 2 * total), bf16),
            pltpu.VMEM((2 * GROUP, total, total), bf16),
            pltpu.VMEM((total * PIECE, width), f32),
            dma((devices,)),
            dma((devices,)),
            dma((blocks,)),
            dma((blocks,)),
            dma((devices,)),
            dma((devices,)),
        ],
        compiler_params=pltpu.CompilerParams(
            collective_id=0, has_side_effects=True, vmem_limit_bytes=32 * 2**20
        ),
    )(*args)
    return out.reshape(total, 1, PIECE, width)


def fits(mesh, act_shape, hidden):
    groups, blocks, slabs = mesh.shape["groups"], mesh.shape["blk"], mesh.shape["chan"] * mesh.shape["pair"]
    rows, cols = act_shape[0] // (groups * blocks), act_shape[1] // slabs
    return (
        (rows, cols) == (CELLS, CELLS)
        and act_shape[2] == hidden == 128
        and blocks * slabs * GROUP == hidden
        and blocks == slabs == PIECE
    )


def solution(mesh):
    specs = (P(("groups", "blk"), ("chan", "pair"), None), P(("groups", "blk"), ("chan", "pair"))) + (P(),) * 7

    def run(*args):
        body = in_one_kernel if fits(mesh, args[0].shape, args[6].shape[0]) else on_device
        return jax.shard_map(
            body,
            mesh=mesh,
            in_specs=specs,
            out_specs=P("groups", ("chan", "pair"), "blk", None),
            check_vma=False,
        )(*args)

    return run
```

```python
import functools

import jax
import jax.numpy as jnp
from jax import lax
from jax.experimental import pallas as pl
from jax.experimental.pallas import tpu as pltpu
from jax.sharding import PartitionSpec as P


def from_behind(value, axis, by):
    count = lax.axis_size(axis)
    return lax.ppermute(value, axis, [(i, (i + by) % count) for i in range(count)])


def norm_axis(values, gain, bias, axis):
    mean = jnp.mean(values, axis=axis, keepdims=True)
    centred = values - mean
    var = jnp.mean(centred * centred, axis=axis, keepdims=True)
    return centred * lax.rsqrt(var + 1e-05) * gain + bias


def on_device(pair_act, pair_mask, in_gain, in_bias, w_proj, w_gate, w_out, out_gain, out_bias):
    rows, cols, width = pair_act.shape
    hidden = w_out.shape[0]
    blocks = lax.axis_size("blk")
    chans = lax.axis_size("chan")
    halves = lax.axis_size("pair")
    normed = norm_axis(pair_act.astype(jnp.float32), in_gain, in_bias, -1).astype(jnp.bfloat16)
    weights = w_proj.reshape(width, 4, hidden)
    proj = jnp.einsum("rkd,dgh->ghrk", normed, weights, preferred_element_type=jnp.float32)
    mask_f = pair_mask.astype(jnp.float32)
    left = (jax.nn.sigmoid(proj[0]) * proj[1] * mask_f).astype(jnp.bfloat16)
    right = (jax.nn.sigmoid(proj[2]) * proj[3] * mask_f).astype(jnp.bfloat16)
    left, right = (
        lax.all_to_all(left, "chan", split_axis=0, concat_axis=2, tiled=True),
        lax.all_to_all(right, "chan", split_axis=0, concat_axis=2, tiled=True),
    )
    subset = left.shape[0]
    me_index = lax.axis_index("blk")
    total = rows * blocks
    zero_index = jnp.zeros((), jnp.int32)

    def place(acc, block, owner):
        part = jnp.einsum("cik,cjk->cij", left, block, preferred_element_type=jnp.float32)
        start = owner * rows
        return lax.dynamic_update_slice(acc, part, (zero_index, zero_index, start))

    acc = jnp.zeros((subset, rows, total), jnp.float32)
    acc = place(acc, right, me_index)

    def both_step(step, carry):
        acc_now, ahead, behind = carry
        ahead = from_behind(ahead, "blk", 1)
        behind = from_behind(behind, "blk", -1)
        acc_now = place(acc_now, ahead, (me_index - step) % blocks)
        acc_now = place(acc_now, behind, (me_index + step) % blocks)
        return (acc_now, ahead, behind)

    acc, ahead, behind = lax.fori_loop(1, (blocks - 1) // 2 + 1, both_step, (acc, right, right))
    ahead = from_behind(ahead, "blk", 1)
    acc = place(acc, ahead, (me_index - blocks // 2) % blocks)
    parts = acc.reshape(subset, rows, chans, halves, cols)
    mine = lax.psum_scatter(parts, "pair", scatter_dimension=3, tiled=True)
    full = lax.all_to_all(mine, "chan", split_axis=2, concat_axis=0, tiled=True)
    full = full.reshape(hidden, rows, cols)
    tri_norm = norm_axis(full, out_gain[:, None, None], out_bias[:, None, None], 0).astype(
        jnp.bfloat16
    )
    linear = jnp.einsum("hrj,hd->rjd", tri_norm, w_out, preferred_element_type=jnp.float32)
    gate = jax.nn.sigmoid(
        jnp.einsum("rjd,de->rje", normed, w_gate, preferred_element_type=jnp.float32)
    )
    update = (gate * linear).astype(jnp.bfloat16).reshape(rows, 1, cols, width)
    return lax.all_to_all(update, "blk", split_axis=2, concat_axis=0, tiled=True)


MESH = pl.DeviceIdType.MESH
CELLS = 16
GROUP = 8
PIECE = 4


def dot(a, b, contract):
    return lax.dot_general(a, b, ((contract[:1], contract[1:]), ((), ())), preferred_element_type=jnp.float32)


def kernel(blocks, chans, halves, *refs):
    sources, out, targets = refs[:9], refs[9], refs[10:19]
    fetched = refs[19]
    (
        swap, normed, cells, pick, sides, sides_in, tri_f, tri, tri_in, squares, rows_out,
        side_send, side_recv, cell_send, cell_recv, tri_send, tri_recv,
    ) = refs[20:]
    act, mask, in_gain, in_bias, w_proj, w_gate, w_out, out_gain, out_bias = targets
    fetches = [
        pltpu.make_async_copy(source, target, fetched.at[n])
        for n, (source, target) in enumerate(zip(sources, targets))
    ]
    for fetch in fetches:
        fetch.start()
    slabs = chans * halves
    blk = lax.axis_index("blk")
    slab = lax.axis_index("chan") * halves + lax.axis_index("pair")
    me = slab * blocks + blk
    others = [(ds, db) for db in range(blocks) for ds in range(slabs)]

    def peer(ds, db):
        s = (slab + ds) % slabs
        b = (blk + db) % blocks
        return s, b, s * blocks + b, {"blk": b, "chan": s // halves, "pair": s % halves}

    barrier = pltpu.get_barrier_semaphore()
    for ds, db in others[1:]:
        pl.semaphore_signal(barrier, inc=1, device_id=peer(ds, db)[3], device_id_type=MESH)

    lanes = CELLS * CELLS
    row = lax.broadcasted_iota(jnp.int32, (CELLS, lanes), 0)
    lane = lax.broadcasted_iota(jnp.int32, (CELLS, lanes), 1)
    spread = jnp.where(lane // CELLS == row, 1.0, 0.0).astype(jnp.bfloat16)
    own_row = lane % CELLS == row
    total = slabs * CELLS
    at = lax.broadcasted_iota(jnp.int32, (lanes, total), 0)
    col = lax.broadcasted_iota(jnp.int32, (lanes, total), 1)
    for s in range(slabs):
        pick[s] = jnp.where(col == at // CELLS + s * CELLS, 1.0, 0.0).astype(jnp.bfloat16)
    moved = (row % GROUP) // 2 * PIECE + row // GROUP * 2 + row % 2
    right_row = lane % CELLS == moved
    for fetch in fetches[:4]:
        fetch.wait()

    x = act[...].astype(jnp.float32)
    mean = jnp.mean(x, axis=-1, keepdims=True)
    centred = x - mean
    var = jnp.mean(centred * centred, axis=-1, keepdims=True)
    x = centred * lax.rsqrt(var + 1e-05) * in_gain[...].reshape(1, 1, -1) + in_bias[...].reshape(1, 1, -1)
    for i in range(CELLS):
        swap[pl.ds(i, CELLS, stride=CELLS), :] = x[i]
    z = swap[...].astype(jnp.bfloat16)
    normed[...] = z.reshape(normed.shape)

    mask_rows = dot(mask[...].astype(jnp.float32).astype(jnp.bfloat16), spread, (1, 0))
    mask_row = jnp.sum(jnp.where(own_row, mask_rows, 0.0), axis=0, keepdims=True)

    fetches[4].wait()
    proj = dot(w_proj[...], z, (0, 1))
    hidden = proj.shape[0] // 4
    left = jax.nn.sigmoid(proj[:hidden]) * proj[hidden:2 * hidden] * mask_row
    right = jax.nn.sigmoid(proj[2 * hidden:3 * hidden]) * proj[3 * hidden:] * mask_row
    groups = hidden // GROUP
    both = jnp.concatenate(
        [left.reshape(groups, GROUP, lanes), right.reshape(groups, GROUP, lanes)], axis=1
    )
    sides[...] = both.astype(jnp.bfloat16)

    pl.semaphore_wait(barrier, len(others) - 1)
    copies = []
    for n, (ds, db) in list(enumerate(others))[:0:-1]:
        _, _, to, device = peer(ds, db)
        copy = pltpu.make_async_remote_copy(
            src_ref=sides.at[to], dst_ref=sides_in.at[me],
            send_sem=side_send.at[n], recv_sem=side_recv.at[me],
            device_id=device, device_id_type=MESH,
        )
        copy.start()
        copies.append(copy)
    for db in range(1, blocks):
        b = (blk + db) % blocks
        copy = pltpu.make_async_remote_copy(
            src_ref=normed.at[pl.ds(b * PIECE, PIECE)], dst_ref=cells.at[blk],
            send_sem=cell_send.at[db], recv_sem=cell_recv.at[blk],
            device_id={"blk": b}, device_id_type=MESH,
        )
        copy.start()
        copies.append(copy)
    sides_in[me] = sides[me]
    cells[blk] = normed[pl.ds(blk * PIECE, PIECE)]

    for fetch in fetches[5:]:
        fetch.wait()
    gain = jnp.transpose(jnp.broadcast_to(out_gain[...].reshape(1, -1), (hidden, hidden))).reshape(groups, GROUP, hidden)
    bias = jnp.transpose(jnp.broadcast_to(out_bias[...].reshape(1, -1), (hidden, hidden))).reshape(groups, GROUP, hidden)

    for db in range(blocks):
        acc = None
        for ds in range(slabs):
            s, b, frm, device = peer(ds, db)
            if (ds, db) != (0, 0):
                pltpu.make_async_remote_copy(
                    src_ref=sides.at[frm], dst_ref=sides_in.at[frm],
                    send_sem=side_send.at[0], recv_sem=side_recv.at[frm],
                    device_id=device, device_id_type=MESH,
                ).wait_recv()
            part = sides_in[frm].astype(jnp.float32)
            part_left = jnp.where(own_row[None], part[:GROUP][:, None, :], 0.0)
            part_right = jnp.where(right_row[None], part[GROUP:][:, None, :], 0.0)
            wide = jnp.concatenate([part_left, part_right], axis=0).reshape(2 * GROUP * CELLS, lanes)
            term = dot(wide.astype(jnp.bfloat16), pick[s], (1, 0))
            acc = term if acc is None else acc + term
        b = (blk + db) % blocks
        rows_of = pl.ds(pl.multiple_of(b * CELLS, CELLS), CELLS)
        block = acc.astype(jnp.bfloat16).reshape(2 * GROUP, CELLS, total)
        squares[:, rows_of, :] = block

    wide_rows = blocks * GROUP
    for h in range(GROUP):
        t = dot(squares[GROUP + h], squares[h], (1, 1)).reshape(blocks, 2, GROUP, total)
        t = jnp.concatenate([t[:, 0], t[:, 1]], axis=-1).reshape(wide_rows, 2 * total)
        tri_f[pl.ds(h, wide_rows, stride=GROUP), :] = t
    tri[...] = tri_f[...].astype(jnp.bfloat16).reshape(tri.shape)

    for n, (ds, db) in list(enumerate(others))[:0:-1]:
        _, _, to, device = peer(ds, db)
        copy = pltpu.make_async_remote_copy(
            src_ref=tri.at[to], dst_ref=tri_in.at[me],
            send_sem=tri_send.at[n], recv_sem=tri_recv.at[me],
            device_id=device, device_id_type=MESH,
        )
        copy.start()
        copies.append(copy)
    tri_in[me] = tri[me]

    for db in range(1, blocks):
        b = (blk + db) % blocks
        pltpu.make_async_remote_copy(
            src_ref=cells.at[b], dst_ref=cells.at[b],
            send_sem=cell_send.at[0], recv_sem=cell_recv.at[b],
            device_id={"blk": b}, device_id_type=MESH,
        ).wait_recv()
    mine = jnp.concatenate([cells[b, m] for m in range(PIECE) for b in range(blocks)], axis=0)
    gate = jax.nn.sigmoid(dot(mine, w_gate[...], (1, 0)))

    for ds, db in others[1:]:
        _, _, frm, device = peer(ds, db)
        pltpu.make_async_remote_copy(
            src_ref=tri.at[frm], dst_ref=tri_in.at[frm],
            send_sem=tri_send.at[0], recv_sem=tri_recv.at[frm],
            device_id=device, device_id_type=MESH,
        ).wait_recv()
    full = tri_in[...].astype(jnp.float32).reshape(groups, 2, GROUP, hidden)
    for q in range(2):
        t = full[:, q]
        mean = jnp.mean(t, axis=(0, 1), keepdims=True)
        centred = t - mean
        var = jnp.mean(centred * centred, axis=(0, 1), keepdims=True)
        t = centred * lax.rsqrt(var + 1e-05) * gain + bias
        linear = dot(t.reshape(hidden, hidden).astype(jnp.bfloat16), w_out[...], (0, 0))
        for p in range(2):
            m = p * 2 + q
            rows_out[pl.ds(m, total, stride=PIECE), :] = linear[p * total:(p + 1) * total] * gate[m * total:(m + 1) * total]
    out[...] = rows_out[...].astype(jnp.bfloat16)
    for copy in copies:
        copy.wait_send()


def in_one_kernel(*args):
    blocks = lax.axis_size("blk")
    chans = lax.axis_size("chan")
    halves = lax.axis_size("pair")
    rows, cols, width = args[0].shape
    slabs = chans * halves
    devices = blocks * slabs
    total = rows * blocks
    bf16, f32 = jnp.bfloat16, jnp.float32
    dma = pltpu.SemaphoreType.DMA
    vmem = pl.BlockSpec(memory_space=pltpu.VMEM)
    out = pl.pallas_call(
        functools.partial(kernel, blocks, chans, halves),
        out_shape=jax.ShapeDtypeStruct((total * PIECE, width), bf16),
        in_specs=[pl.BlockSpec(memory_space=pltpu.HBM)] * len(args),
        out_specs=vmem,
        scratch_shapes=[pltpu.VMEM(a.shape, a.dtype) for a in args] + [
            dma((len(args),)),
            pltpu.VMEM((rows * cols, width), f32),
            pltpu.VMEM((cols, rows, width), bf16),
            pltpu.VMEM((blocks, PIECE, rows, width), bf16),
            pltpu.VMEM((slabs, rows * cols, total), bf16),
            pltpu.VMEM((devices, 2 * GROUP, rows * cols), bf16),
            pltpu.VMEM((devices, 2 * GROUP, rows * cols), bf16),
            pltpu.VMEM((devices * 2 * GROUP, 2 * total), f32),
            pltpu.VMEM((devices, 2 * GROUP, 2 * total), bf16),
            pltpu.VMEM((devices, 2 * GROUP, 2 * total), bf16),
            pltpu.VMEM((2 * GROUP, total, total), bf16),
            pltpu.VMEM((total * PIECE, width), f32),
            dma((devices,)),
            dma((devices,)),
            dma((blocks,)),
            dma((blocks,)),
            dma((devices,)),
            dma((devices,)),
        ],
        compiler_params=pltpu.CompilerParams(
            collective_id=0, has_side_effects=True, vmem_limit_bytes=64 * 2**20
        ),
    )(*args)
    return out.reshape(total, 1, PIECE, width)


def fits(mesh, act_shape, hidden):
    groups, blocks, slabs = mesh.shape["groups"], mesh.shape["blk"], mesh.shape["chan"] * mesh.shape["pair"]
    rows, cols = act_shape[0] // (groups * blocks), act_shape[1] // slabs
    return (
        (rows, cols) == (CELLS, CELLS)
        and act_shape[2] == hidden == 128
        and blocks * slabs * GROUP == hidden
        and blocks == slabs == PIECE
    )


def solution(mesh):
    specs = (P(("groups", "blk"), ("chan", "pair"), None), P(("groups", "blk"), ("chan", "pair"))) + (P(),) * 7

    def run(*args):
        body = in_one_kernel if fits(mesh, args[0].shape, args[6].shape[0]) else on_device
        return jax.shard_map(
            body,
            mesh=mesh,
            in_specs=specs,
            out_specs=P("groups", ("chan", "pair"), "blk", None),
            check_vma=False,
        )(*args)

    return run
```

```python
import functools

import jax
import jax.numpy as jnp
from jax import lax
from jax.experimental import pallas as pl
from jax.experimental.pallas import tpu as pltpu
from jax.sharding import PartitionSpec as P


def from_behind(value, axis, by):
    count = lax.axis_size(axis)
    return lax.ppermute(value, axis, [(i, (i + by) % count) for i in range(count)])


def norm_axis(values, gain, bias, axis):
    mean = jnp.mean(values, axis=axis, keepdims=True)
    centred = values - mean
    var = jnp.mean(centred * centred, axis=axis, keepdims=True)
    return centred * lax.rsqrt(var + 1e-05) * gain + bias


def on_device(pair_act, pair_mask, in_gain, in_bias, w_proj, w_gate, w_out, out_gain, out_bias):
    rows, cols, width = pair_act.shape
    hidden = w_out.shape[0]
    blocks = lax.axis_size("blk")
    chans = lax.axis_size("chan")
    halves = lax.axis_size("pair")
    normed = norm_axis(pair_act.astype(jnp.float32), in_gain, in_bias, -1).astype(jnp.bfloat16)
    weights = w_proj.reshape(width, 4, hidden)
    proj = jnp.einsum("rkd,dgh->ghrk", normed, weights, preferred_element_type=jnp.float32)
    mask_f = pair_mask.astype(jnp.float32)
    left = (jax.nn.sigmoid(proj[0]) * proj[1] * mask_f).astype(jnp.bfloat16)
    right = (jax.nn.sigmoid(proj[2]) * proj[3] * mask_f).astype(jnp.bfloat16)
    left, right = (
        lax.all_to_all(left, "chan", split_axis=0, concat_axis=2, tiled=True),
        lax.all_to_all(right, "chan", split_axis=0, concat_axis=2, tiled=True),
    )
    subset = left.shape[0]
    me_index = lax.axis_index("blk")
    total = rows * blocks
    zero_index = jnp.zeros((), jnp.int32)

    def place(acc, block, owner):
        part = jnp.einsum("cik,cjk->cij", left, block, preferred_element_type=jnp.float32)
        start = owner * rows
        return lax.dynamic_update_slice(acc, part, (zero_index, zero_index, start))

    acc = jnp.zeros((subset, rows, total), jnp.float32)
    acc = place(acc, right, me_index)

    def both_step(step, carry):
        acc_now, ahead, behind = carry
        ahead = from_behind(ahead, "blk", 1)
        behind = from_behind(behind, "blk", -1)
        acc_now = place(acc_now, ahead, (me_index - step) % blocks)
        acc_now = place(acc_now, behind, (me_index + step) % blocks)
        return (acc_now, ahead, behind)

    acc, ahead, behind = lax.fori_loop(1, (blocks - 1) // 2 + 1, both_step, (acc, right, right))
    ahead = from_behind(ahead, "blk", 1)
    acc = place(acc, ahead, (me_index - blocks // 2) % blocks)
    parts = acc.reshape(subset, rows, chans, halves, cols)
    mine = lax.psum_scatter(parts, "pair", scatter_dimension=3, tiled=True)
    full = lax.all_to_all(mine, "chan", split_axis=2, concat_axis=0, tiled=True)
    full = full.reshape(hidden, rows, cols)
    tri_norm = norm_axis(full, out_gain[:, None, None], out_bias[:, None, None], 0).astype(
        jnp.bfloat16
    )
    linear = jnp.einsum("hrj,hd->rjd", tri_norm, w_out, preferred_element_type=jnp.float32)
    gate = jax.nn.sigmoid(
        jnp.einsum("rjd,de->rje", normed, w_gate, preferred_element_type=jnp.float32)
    )
    update = (gate * linear).astype(jnp.bfloat16).reshape(rows, 1, cols, width)
    return lax.all_to_all(update, "blk", split_axis=2, concat_axis=0, tiled=True)


MESH = pl.DeviceIdType.MESH
CELLS = 16
GROUP = 8
PIECE = 4


def dot(a, b, contract):
    return lax.dot_general(a, b, ((contract[:1], contract[1:]), ((), ())), preferred_element_type=jnp.float32)


def kernel(blocks, chans, halves, *refs):
    sources, out, targets = refs[:9], refs[9], refs[10:19]
    fetched = refs[19]
    (
        swap, normed, cells, pick, sides, sides_in, tri_f, tri, tri_in, squares, rows_out,
        side_send, side_recv, cell_send, cell_recv, tri_send, tri_recv,
    ) = refs[20:]
    act, mask, in_gain, in_bias, w_proj, w_gate, w_out, out_gain, out_bias = targets
    fetches = [
        pltpu.make_async_copy(source, target, fetched.at[n])
        for n, (source, target) in enumerate(zip(sources, targets))
    ]
    for fetch in fetches:
        fetch.start()
    slabs = chans * halves
    blk = lax.axis_index("blk")
    slab = lax.axis_index("chan") * halves + lax.axis_index("pair")
    me = slab * blocks + blk
    others = [(ds, db) for db in range(blocks) for ds in range(slabs)]

    def peer(ds, db):
        s = (slab + ds) % slabs
        b = (blk + db) % blocks
        return s, b, s * blocks + b, {"blk": b, "chan": s // halves, "pair": s % halves}

    barrier = pltpu.get_barrier_semaphore()
    for ds, db in others[1:]:
        pl.semaphore_signal(barrier, inc=1, device_id=peer(ds, db)[3], device_id_type=MESH)

    lanes = CELLS * CELLS
    row = lax.broadcasted_iota(jnp.int32, (CELLS, lanes), 0)
    lane = lax.broadcasted_iota(jnp.int32, (CELLS, lanes), 1)
    spread = jnp.where(lane // CELLS == row, 1.0, 0.0).astype(jnp.bfloat16)
    own_row = lane % CELLS == row
    total = slabs * CELLS
    at = lax.broadcasted_iota(jnp.int32, (lanes, total), 0)
    col = lax.broadcasted_iota(jnp.int32, (lanes, total), 1)
    for s in range(slabs):
        pick[s] = jnp.where(col == at // CELLS + s * CELLS, 1.0, 0.0).astype(jnp.bfloat16)
    moved = (row % GROUP) // 2 * PIECE + row // GROUP * 2 + row % 2
    right_row = lane % CELLS == moved
    for fetch in fetches[:4]:
        fetch.wait()

    x = act[...].astype(jnp.float32)
    mean = jnp.mean(x, axis=-1, keepdims=True)
    centred = x - mean
    var = jnp.mean(centred * centred, axis=-1, keepdims=True)
    x = centred * lax.rsqrt(var + 1e-05) * in_gain[...].reshape(1, 1, -1) + in_bias[...].reshape(1, 1, -1)
    for i in range(CELLS):
        swap[pl.ds(i, CELLS, stride=CELLS), :] = x[i]
    z = swap[...].astype(jnp.bfloat16)
    normed[...] = z.reshape(normed.shape)

    mask_rows = dot(mask[...].astype(jnp.float32).astype(jnp.bfloat16), spread, (1, 0))
    mask_row = jnp.sum(jnp.where(own_row, mask_rows, 0.0), axis=0, keepdims=True)

    fetches[4].wait()
    proj = dot(w_proj[...], z, (0, 1))
    hidden = proj.shape[0] // 4
    left = jax.nn.sigmoid(proj[:hidden]) * proj[hidden:2 * hidden] * mask_row
    right = jax.nn.sigmoid(proj[2 * hidden:3 * hidden]) * proj[3 * hidden:] * mask_row
    groups = hidden // GROUP
    both = jnp.concatenate(
        [left.reshape(groups, GROUP, lanes), right.reshape(groups, GROUP, lanes)], axis=1
    )
    sides[...] = both.astype(jnp.bfloat16)

    pl.semaphore_wait(barrier, len(others) - 1)
    copies = []
    for n, (ds, db) in list(enumerate(others))[:0:-1]:
        _, _, to, device = peer(ds, db)
        copy = pltpu.make_async_remote_copy(
            src_ref=sides.at[to], dst_ref=sides_in.at[me],
            send_sem=side_send.at[n], recv_sem=side_recv.at[me],
            device_id=device, device_id_type=MESH,
        )
        copy.start()
        copies.append(copy)
    for db in range(1, blocks):
        b = (blk + db) % blocks
        copy = pltpu.make_async_remote_copy(
            src_ref=normed.at[pl.ds(b * PIECE, PIECE)], dst_ref=cells.at[blk],
            send_sem=cell_send.at[db], recv_sem=cell_recv.at[blk],
            device_id={"blk": b}, device_id_type=MESH,
        )
        copy.start()
        copies.append(copy)
    sides_in[me] = sides[me]
    cells[blk] = normed[pl.ds(blk * PIECE, PIECE)]

    for fetch in fetches[5:]:
        fetch.wait()
    gain = jnp.transpose(jnp.broadcast_to(out_gain[...].reshape(1, -1), (hidden, hidden))).reshape(groups, GROUP, hidden)
    bias = jnp.transpose(jnp.broadcast_to(out_bias[...].reshape(1, -1), (hidden, hidden))).reshape(groups, GROUP, hidden)

    for db in range(blocks):
        acc = None
        for ds in range(slabs):
            s, b, frm, device = peer(ds, db)
            if (ds, db) != (0, 0):
                pltpu.make_async_remote_copy(
                    src_ref=sides.at[frm], dst_ref=sides_in.at[frm],
                    send_sem=side_send.at[0], recv_sem=side_recv.at[frm],
                    device_id=device, device_id_type=MESH,
                ).wait_recv()
            part = sides_in[frm].astype(jnp.float32)
            part_left = jnp.where(own_row[None], part[:GROUP][:, None, :], 0.0)
            part_right = jnp.where(right_row[None], part[GROUP:][:, None, :], 0.0)
            wide = jnp.concatenate([part_left, part_right], axis=0).reshape(2 * GROUP * CELLS, lanes)
            term = dot(wide.astype(jnp.bfloat16), pick[s], (1, 0))
            acc = term if acc is None else acc + term
        b = (blk + db) % blocks
        rows_of = pl.ds(pl.multiple_of(b * CELLS, CELLS), CELLS)
        block = acc.astype(jnp.bfloat16).reshape(2 * GROUP, CELLS, total)
        squares[:, rows_of, :] = block

    wide_rows = blocks * GROUP
    for h in range(GROUP):
        t = dot(squares[GROUP + h], squares[h], (1, 1)).reshape(blocks, 2, GROUP, total)
        t = jnp.concatenate([t[:, 0], t[:, 1]], axis=-1).reshape(wide_rows, 2 * total)
        tri_f[pl.ds(h, wide_rows, stride=GROUP), :] = t
    tri[...] = tri_f[...].astype(jnp.bfloat16).reshape(tri.shape)

    for n, (ds, db) in list(enumerate(others))[:0:-1]:
        _, _, to, device = peer(ds, db)
        copy = pltpu.make_async_remote_copy(
            src_ref=tri.at[to], dst_ref=tri_in.at[me],
            send_sem=tri_send.at[n], recv_sem=tri_recv.at[me],
            device_id=device, device_id_type=MESH,
        )
        copy.start()
        copies.append(copy)
    tri_in[me] = tri[me]

    for db in range(1, blocks):
        b = (blk + db) % blocks
        pltpu.make_async_remote_copy(
            src_ref=cells.at[b], dst_ref=cells.at[b],
            send_sem=cell_send.at[0], recv_sem=cell_recv.at[b],
            device_id={"blk": b}, device_id_type=MESH,
        ).wait_recv()
    mine = jnp.concatenate([cells[b, m] for m in range(PIECE) for b in range(blocks)], axis=0)
    gate = jax.nn.sigmoid(dot(mine, w_gate[...], (1, 0)))

    for ds, db in others[1:]:
        _, _, frm, device = peer(ds, db)
        pltpu.make_async_remote_copy(
            src_ref=tri.at[frm], dst_ref=tri_in.at[frm],
            send_sem=tri_send.at[0], recv_sem=tri_recv.at[frm],
            device_id=device, device_id_type=MESH,
        ).wait_recv()
    full = tri_in[...].astype(jnp.float32).reshape(groups, 2, GROUP, hidden)
    for q in range(2):
        t = full[:, q]
        mean = jnp.mean(t, axis=(0, 1), keepdims=True)
        centred = t - mean
        var = jnp.mean(centred * centred, axis=(0, 1), keepdims=True)
        t = centred * lax.rsqrt(var + 1e-05) * gain + bias
        linear = dot(t.reshape(hidden, hidden).astype(jnp.bfloat16), w_out[...], (0, 0))
        for p in range(2):
            m = p * 2 + q
            rows_out[pl.ds(m, total, stride=PIECE), :] = linear[p * total:(p + 1) * total] * gate[m * total:(m + 1) * total]
    out[...] = rows_out[...].astype(jnp.bfloat16)
    for copy in copies:
        copy.wait_send()


def in_one_kernel(*args):
    blocks = lax.axis_size("blk")
    chans = lax.axis_size("chan")
    halves = lax.axis_size("pair")
    rows, cols, width = args[0].shape
    slabs = chans * halves
    devices = blocks * slabs
    total = rows * blocks
    bf16, f32 = jnp.bfloat16, jnp.float32
    dma = pltpu.SemaphoreType.DMA
    vmem = pl.BlockSpec(memory_space=pltpu.VMEM)
    out = pl.pallas_call(
        functools.partial(kernel, blocks, chans, halves),
        out_shape=pltpu.VMEM((total * PIECE, width), bf16),
        in_specs=[pl.BlockSpec(memory_space=pltpu.HBM)] * len(args),
        out_specs=vmem,
        scratch_shapes=[pltpu.VMEM(a.shape, a.dtype) for a in args] + [
            dma((len(args),)),
            pltpu.VMEM((rows * cols, width), f32),
            pltpu.VMEM((cols, rows, width), bf16),
            pltpu.VMEM((blocks, PIECE, rows, width), bf16),
            pltpu.VMEM((slabs, rows * cols, total), bf16),
            pltpu.VMEM((devices, 2 * GROUP, rows * cols), bf16),
            pltpu.VMEM((devices, 2 * GROUP, rows * cols), bf16),
            pltpu.VMEM((devices * 2 * GROUP, 2 * total), f32),
            pltpu.VMEM((devices, 2 * GROUP, 2 * total), bf16),
            pltpu.VMEM((devices, 2 * GROUP, 2 * total), bf16),
            pltpu.VMEM((2 * GROUP, total, total), bf16),
            pltpu.VMEM((total * PIECE, width), f32),
            dma((devices,)),
            dma((devices,)),
            dma((blocks,)),
            dma((blocks,)),
            dma((devices,)),
            dma((devices,)),
        ],
        compiler_params=pltpu.CompilerParams(
            collective_id=0, has_side_effects=True, vmem_limit_bytes=60 * 2**20
        ),
    )(*args)
    return out.reshape(total, 1, PIECE, width)


def fits(mesh, act_shape, hidden):
    groups, blocks, slabs = mesh.shape["groups"], mesh.shape["blk"], mesh.shape["chan"] * mesh.shape["pair"]
    rows, cols = act_shape[0] // (groups * blocks), act_shape[1] // slabs
    return (
        (rows, cols) == (CELLS, CELLS)
        and act_shape[2] == hidden == 128
        and blocks * slabs * GROUP == hidden
        and blocks == slabs == PIECE
    )


def solution(mesh):
    specs = (P(("groups", "blk"), ("chan", "pair"), None), P(("groups", "blk"), ("chan", "pair"))) + (P(),) * 7

    def run(*args):
        body = in_one_kernel if fits(mesh, args[0].shape, args[6].shape[0]) else on_device
        return jax.shard_map(
            body,
            mesh=mesh,
            in_specs=specs,
            out_specs=P("groups", ("chan", "pair"), "blk", None),
            check_vma=False,
        )(*args)

    return run
```

```python
import functools

import jax
import jax.numpy as jnp
from jax import lax
from jax.experimental import pallas as pl
from jax.experimental.pallas import tpu as pltpu
from jax.sharding import PartitionSpec as P


def from_behind(value, axis, by):
    count = lax.axis_size(axis)
    return lax.ppermute(value, axis, [(i, (i + by) % count) for i in range(count)])


def norm_axis(values, gain, bias, axis):
    mean = jnp.mean(values, axis=axis, keepdims=True)
    centred = values - mean
    var = jnp.mean(centred * centred, axis=axis, keepdims=True)
    return centred * lax.rsqrt(var + 1e-05) * gain + bias


def on_device(pair_act, pair_mask, in_gain, in_bias, w_proj, w_gate, w_out, out_gain, out_bias):
    rows, cols, width = pair_act.shape
    hidden = w_out.shape[0]
    blocks = lax.axis_size("blk")
    chans = lax.axis_size("chan")
    halves = lax.axis_size("pair")
    normed = norm_axis(pair_act.astype(jnp.float32), in_gain, in_bias, -1).astype(jnp.bfloat16)
    weights = w_proj.reshape(width, 4, hidden)
    proj = jnp.einsum("rkd,dgh->ghrk", normed, weights, preferred_element_type=jnp.float32)
    mask_f = pair_mask.astype(jnp.float32)
    left = (jax.nn.sigmoid(proj[0]) * proj[1] * mask_f).astype(jnp.bfloat16)
    right = (jax.nn.sigmoid(proj[2]) * proj[3] * mask_f).astype(jnp.bfloat16)
    left, right = (
        lax.all_to_all(left, "chan", split_axis=0, concat_axis=2, tiled=True),
        lax.all_to_all(right, "chan", split_axis=0, concat_axis=2, tiled=True),
    )
    subset = left.shape[0]
    me_index = lax.axis_index("blk")
    total = rows * blocks
    zero_index = jnp.zeros((), jnp.int32)

    def place(acc, block, owner):
        part = jnp.einsum("cik,cjk->cij", left, block, preferred_element_type=jnp.float32)
        start = owner * rows
        return lax.dynamic_update_slice(acc, part, (zero_index, zero_index, start))

    acc = jnp.zeros((subset, rows, total), jnp.float32)
    acc = place(acc, right, me_index)

    def both_step(step, carry):
        acc_now, ahead, behind = carry
        ahead = from_behind(ahead, "blk", 1)
        behind = from_behind(behind, "blk", -1)
        acc_now = place(acc_now, ahead, (me_index - step) % blocks)
        acc_now = place(acc_now, behind, (me_index + step) % blocks)
        return (acc_now, ahead, behind)

    acc, ahead, behind = lax.fori_loop(1, (blocks - 1) // 2 + 1, both_step, (acc, right, right))
    ahead = from_behind(ahead, "blk", 1)
    acc = place(acc, ahead, (me_index - blocks // 2) % blocks)
    parts = acc.reshape(subset, rows, chans, halves, cols)
    mine = lax.psum_scatter(parts, "pair", scatter_dimension=3, tiled=True)
    full = lax.all_to_all(mine, "chan", split_axis=2, concat_axis=0, tiled=True)
    full = full.reshape(hidden, rows, cols)
    tri_norm = norm_axis(full, out_gain[:, None, None], out_bias[:, None, None], 0).astype(
        jnp.bfloat16
    )
    linear = jnp.einsum("hrj,hd->rjd", tri_norm, w_out, preferred_element_type=jnp.float32)
    gate = jax.nn.sigmoid(
        jnp.einsum("rjd,de->rje", normed, w_gate, preferred_element_type=jnp.float32)
    )
    update = (gate * linear).astype(jnp.bfloat16).reshape(rows, 1, cols, width)
    return lax.all_to_all(update, "blk", split_axis=2, concat_axis=0, tiled=True)


MESH = pl.DeviceIdType.MESH
CELLS = 16
GROUP = 8
PIECE = 4


def dot(a, b, contract):
    return lax.dot_general(a, b, ((contract[:1], contract[1:]), ((), ())), preferred_element_type=jnp.float32)


def kernel(blocks, chans, halves, *refs):
    sources, out, targets = refs[:9], refs[9], refs[10:19]
    fetched = refs[19]
    (
        swap, normed, cells, pick, sides, sides_in, tri_f, tri, tri_in, squares, rows_out,
        side_send, side_recv, cell_send, cell_recv, tri_send, tri_recv,
    ) = refs[20:]
    act, mask, in_gain, in_bias, w_proj, w_gate, w_out, out_gain, out_bias = targets
    fetches = [
        pltpu.make_async_copy(source, target, fetched.at[n])
        for n, (source, target) in enumerate(zip(sources, targets))
    ]
    for fetch in fetches:
        fetch.start()
    slabs = chans * halves
    devices = blocks * slabs
    blk = lax.axis_index("blk")
    chan = lax.axis_index("chan")
    half = lax.axis_index("pair")
    slab = chan * halves + half
    me = slab * blocks + blk
    blks = (blk, blk + 1 - 2 * (blk % 2), (blk + 2) % 4, 3 - blk)
    chan_of = (chan, 1 - chan)
    half_of = (half, 1 - half)

    def peer(n):
        b, c, p = blks[n // 4], chan_of[n // 2 % 2], half_of[n % 2]
        s = c * halves + p
        return s, b, s * blocks + b, {"blk": b, "chan": c, "pair": p}

    barrier = pltpu.get_barrier_semaphore()
    for n in range(1, devices):
        pl.semaphore_signal(barrier, inc=1, device_id=peer(n)[3], device_id_type=MESH)

    lanes = CELLS * CELLS
    row = lax.broadcasted_iota(jnp.int32, (CELLS, lanes), 0)
    lane = lax.broadcasted_iota(jnp.int32, (CELLS, lanes), 1)
    spread = jnp.where(lane // CELLS == row, 1.0, 0.0).astype(jnp.bfloat16)
    own_row = lane % CELLS == row
    total = slabs * CELLS
    at = lax.broadcasted_iota(jnp.int32, (lanes, total), 0)
    col = lax.broadcasted_iota(jnp.int32, (lanes, total), 1)
    for s in range(slabs):
        pick[s] = jnp.where(col == at // CELLS + s * CELLS, 1.0, 0.0).astype(jnp.bfloat16)
    moved = (row % GROUP) // 2 * PIECE + row // GROUP * 2 + row % 2
    right_row = lane % CELLS == moved
    for fetch in fetches[:4]:
        fetch.wait()

    x = act[...].astype(jnp.float32)
    mean = jnp.mean(x, axis=-1, keepdims=True)
    centred = x - mean
    var = jnp.mean(centred * centred, axis=-1, keepdims=True)
    x = centred * lax.rsqrt(var + 1e-05) * in_gain[...].reshape(1, 1, -1) + in_bias[...].reshape(1, 1, -1)
    for i in range(CELLS):
        swap[pl.ds(i, CELLS, stride=CELLS), :] = x[i]
    z = swap[...].astype(jnp.bfloat16)
    normed[...] = z.reshape(normed.shape)

    mask_rows = dot(mask[...].astype(jnp.float32).astype(jnp.bfloat16), spread, (1, 0))
    mask_row = jnp.sum(jnp.where(own_row, mask_rows, 0.0), axis=0, keepdims=True)

    fetches[4].wait()
    proj = dot(w_proj[...], z, (0, 1))
    hidden = proj.shape[0] // 4
    left = jax.nn.sigmoid(proj[:hidden]) * proj[hidden:2 * hidden] * mask_row
    right = jax.nn.sigmoid(proj[2 * hidden:3 * hidden]) * proj[3 * hidden:] * mask_row
    groups = hidden // GROUP
    both = jnp.concatenate(
        [left.reshape(groups, GROUP, lanes), right.reshape(groups, GROUP, lanes)], axis=1
    )
    sides[...] = both.astype(jnp.bfloat16)

    pl.semaphore_wait(barrier, devices - 1)
    copies = []
    for n in range(devices - 1, 0, -1):
        _, _, to, device = peer(n)
        copy = pltpu.make_async_remote_copy(
            src_ref=sides.at[to], dst_ref=sides_in.at[n],
            send_sem=side_send.at[n], recv_sem=side_recv.at[n],
            device_id=device, device_id_type=MESH,
        )
        copy.start()
        copies.append(copy)
    for n in range(1, blocks):
        b = blks[n]
        copy = pltpu.make_async_remote_copy(
            src_ref=normed.at[pl.ds(b * PIECE, PIECE)], dst_ref=cells.at[blk],
            send_sem=cell_send.at[n], recv_sem=cell_recv.at[n],
            device_id={"blk": b}, device_id_type=MESH,
        )
        copy.start()
        copies.append(copy)
    sides_in[0] = sides[me]
    cells[blk] = normed[pl.ds(blk * PIECE, PIECE)]

    for fetch in fetches[5:]:
        fetch.wait()
    gain = jnp.transpose(jnp.broadcast_to(out_gain[...].reshape(1, -1), (hidden, hidden))).reshape(groups, GROUP, hidden)
    bias = jnp.transpose(jnp.broadcast_to(out_bias[...].reshape(1, -1), (hidden, hidden))).reshape(groups, GROUP, hidden)

    for nb in range(blocks):
        acc = None
        for n in range(nb * slabs, nb * slabs + slabs):
            s, b, frm, device = peer(n)
            if n:
                pltpu.make_async_remote_copy(
                    src_ref=sides.at[frm], dst_ref=sides_in.at[n],
                    send_sem=side_send.at[n], recv_sem=side_recv.at[n],
                    device_id=device, device_id_type=MESH,
                ).wait_recv()
            part = sides_in[n].astype(jnp.float32)
            part_left = jnp.where(own_row[None], part[:GROUP][:, None, :], 0.0)
            part_right = jnp.where(right_row[None], part[GROUP:][:, None, :], 0.0)
            wide = jnp.concatenate([part_left, part_right], axis=0).reshape(2 * GROUP * CELLS, lanes)
            term = dot(wide.astype(jnp.bfloat16), pick[s], (1, 0))
            acc = term if acc is None else acc + term
        rows_of = pl.ds(pl.multiple_of(b * CELLS, CELLS), CELLS)
        block = acc.astype(jnp.bfloat16).reshape(2 * GROUP, CELLS, total)
        squares[:, rows_of, :] = block

    wide_rows = blocks * GROUP
    for h in range(GROUP):
        t = dot(squares[GROUP + h], squares[h], (1, 1)).reshape(blocks, 2, GROUP, total)
        t = jnp.concatenate([t[:, 0], t[:, 1]], axis=-1).reshape(wide_rows, 2 * total)
        tri_f[pl.ds(h, wide_rows, stride=GROUP), :] = t
    tri[...] = tri_f[...].astype(jnp.bfloat16).reshape(tri.shape)

    for n in range(devices - 1, 0, -1):
        _, _, to, device = peer(n)
        copy = pltpu.make_async_remote_copy(
            src_ref=tri.at[to], dst_ref=tri_in.at[me],
            send_sem=tri_send.at[n], recv_sem=tri_recv.at[n],
            device_id=device, device_id_type=MESH,
        )
        copy.start()
        copies.append(copy)
    tri_in[me] = tri[me]

    for n in range(1, blocks):
        b = blks[n]
        pltpu.make_async_remote_copy(
            src_ref=cells.at[b], dst_ref=cells.at[b],
            send_sem=cell_send.at[n], recv_sem=cell_recv.at[n],
            device_id={"blk": b}, device_id_type=MESH,
        ).wait_recv()
    mine = jnp.concatenate([cells[b, m] for m in range(PIECE) for b in range(blocks)], axis=0)
    gate = jax.nn.sigmoid(dot(mine, w_gate[...], (1, 0)))

    for n in range(1, devices):
        _, _, frm, device = peer(n)
        pltpu.make_async_remote_copy(
            src_ref=tri.at[frm], dst_ref=tri_in.at[frm],
            send_sem=tri_send.at[n], recv_sem=tri_recv.at[n],
            device_id=device, device_id_type=MESH,
        ).wait_recv()
    full = tri_in[...].astype(jnp.float32).reshape(groups, 2, GROUP, hidden)
    for q in range(2):
        t = full[:, q]
        mean = jnp.mean(t, axis=(0, 1), keepdims=True)
        centred = t - mean
        var = jnp.mean(centred * centred, axis=(0, 1), keepdims=True)
        t = centred * lax.rsqrt(var + 1e-05) * gain + bias
        linear = dot(t.reshape(hidden, hidden).astype(jnp.bfloat16), w_out[...], (0, 0))
        for p in range(2):
            m = p * 2 + q
            rows_out[pl.ds(m, total, stride=PIECE), :] = linear[p * total:(p + 1) * total] * gate[m * total:(m + 1) * total]
    out[...] = rows_out[...].astype(jnp.bfloat16)
    for copy in copies:
        copy.wait_send()


def in_one_kernel(*args):
    blocks = lax.axis_size("blk")
    chans = lax.axis_size("chan")
    halves = lax.axis_size("pair")
    rows, cols, width = args[0].shape
    slabs = chans * halves
    devices = blocks * slabs
    total = rows * blocks
    bf16, f32 = jnp.bfloat16, jnp.float32
    dma = pltpu.SemaphoreType.DMA
    vmem = pl.BlockSpec(memory_space=pltpu.VMEM)
    out = pl.pallas_call(
        functools.partial(kernel, blocks, chans, halves),
        out_shape=pltpu.VMEM((total * PIECE, width), bf16),
        in_specs=[pl.BlockSpec(memory_space=pltpu.HBM)] * len(args),
        out_specs=vmem,
        scratch_shapes=[pltpu.VMEM(a.shape, a.dtype) for a in args] + [
            dma((len(args),)),
            pltpu.VMEM((rows * cols, width), f32),
            pltpu.VMEM((cols, rows, width), bf16),
            pltpu.VMEM((blocks, PIECE, rows, width), bf16),
            pltpu.VMEM((slabs, rows * cols, total), bf16),
            pltpu.VMEM((devices, 2 * GROUP, rows * cols), bf16),
            pltpu.VMEM((devices, 2 * GROUP, rows * cols), bf16),
            pltpu.VMEM((devices * 2 * GROUP, 2 * total), f32),
            pltpu.VMEM((devices, 2 * GROUP, 2 * total), bf16),
            pltpu.VMEM((devices, 2 * GROUP, 2 * total), bf16),
            pltpu.VMEM((2 * GROUP, total, total), bf16),
            pltpu.VMEM((total * PIECE, width), f32),
            dma((devices,)),
            dma((devices,)),
            dma((blocks,)),
            dma((blocks,)),
            dma((devices,)),
            dma((devices,)),
        ],
        compiler_params=pltpu.CompilerParams(
            collective_id=0, has_side_effects=True, vmem_limit_bytes=60 * 2**20
        ),
    )(*args)
    return out.reshape(total, 1, PIECE, width)


def fits(mesh, act_shape, hidden):
    groups, blocks, chans, halves = (mesh.shape[a] for a in ("groups", "blk", "chan", "pair"))
    slabs = chans * halves
    rows, cols = act_shape[0] // (groups * blocks), act_shape[1] // slabs
    return (
        (rows, cols) == (CELLS, CELLS)
        and act_shape[2] == hidden == 128
        and blocks * slabs * GROUP == hidden
        and (blocks, chans, halves) == (4, 2, 2)
    )


def solution(mesh):
    specs = (P(("groups", "blk"), ("chan", "pair"), None), P(("groups", "blk"), ("chan", "pair"))) + (P(),) * 7

    def run(*args):
        body = in_one_kernel if fits(mesh, args[0].shape, args[6].shape[0]) else on_device
        return jax.shard_map(
            body,
            mesh=mesh,
            in_specs=specs,
            out_specs=P("groups", ("chan", "pair"), "blk", None),
            check_vma=False,
        )(*args)

    return run
```

```python
import functools

import jax
import jax.numpy as jnp
from jax import lax
from jax.experimental import pallas as pl
from jax.experimental.pallas import tpu as pltpu
from jax.sharding import PartitionSpec as P


def from_behind(value, axis, by):
    count = lax.axis_size(axis)
    return lax.ppermute(value, axis, [(i, (i + by) % count) for i in range(count)])


def norm_axis(values, gain, bias, axis):
    mean = jnp.mean(values, axis=axis, keepdims=True)
    centred = values - mean
    var = jnp.mean(centred * centred, axis=axis, keepdims=True)
    return centred * lax.rsqrt(var + 1e-05) * gain + bias


def on_device(pair_act, pair_mask, in_gain, in_bias, w_proj, w_gate, w_out, out_gain, out_bias):
    rows, cols, width = pair_act.shape
    hidden = w_out.shape[0]
    blocks = lax.axis_size("blk")
    chans = lax.axis_size("chan")
    halves = lax.axis_size("pair")
    normed = norm_axis(pair_act.astype(jnp.float32), in_gain, in_bias, -1).astype(jnp.bfloat16)
    weights = w_proj.reshape(width, 4, hidden)
    proj = jnp.einsum("rkd,dgh->ghrk", normed, weights, preferred_element_type=jnp.float32)
    mask_f = pair_mask.astype(jnp.float32)
    left = (jax.nn.sigmoid(proj[0]) * proj[1] * mask_f).astype(jnp.bfloat16)
    right = (jax.nn.sigmoid(proj[2]) * proj[3] * mask_f).astype(jnp.bfloat16)
    left, right = (
        lax.all_to_all(left, "chan", split_axis=0, concat_axis=2, tiled=True),
        lax.all_to_all(right, "chan", split_axis=0, concat_axis=2, tiled=True),
    )
    subset = left.shape[0]
    me_index = lax.axis_index("blk")
    total = rows * blocks
    zero_index = jnp.zeros((), jnp.int32)

    def place(acc, block, owner):
        part = jnp.einsum("cik,cjk->cij", left, block, preferred_element_type=jnp.float32)
        start = owner * rows
        return lax.dynamic_update_slice(acc, part, (zero_index, zero_index, start))

    acc = jnp.zeros((subset, rows, total), jnp.float32)
    acc = place(acc, right, me_index)

    def both_step(step, carry):
        acc_now, ahead, behind = carry
        ahead = from_behind(ahead, "blk", 1)
        behind = from_behind(behind, "blk", -1)
        acc_now = place(acc_now, ahead, (me_index - step) % blocks)
        acc_now = place(acc_now, behind, (me_index + step) % blocks)
        return (acc_now, ahead, behind)

    acc, ahead, behind = lax.fori_loop(1, (blocks - 1) // 2 + 1, both_step, (acc, right, right))
    ahead = from_behind(ahead, "blk", 1)
    acc = place(acc, ahead, (me_index - blocks // 2) % blocks)
    parts = acc.reshape(subset, rows, chans, halves, cols)
    mine = lax.psum_scatter(parts, "pair", scatter_dimension=3, tiled=True)
    full = lax.all_to_all(mine, "chan", split_axis=2, concat_axis=0, tiled=True)
    full = full.reshape(hidden, rows, cols)
    tri_norm = norm_axis(full, out_gain[:, None, None], out_bias[:, None, None], 0).astype(
        jnp.bfloat16
    )
    linear = jnp.einsum("hrj,hd->rjd", tri_norm, w_out, preferred_element_type=jnp.float32)
    gate = jax.nn.sigmoid(
        jnp.einsum("rjd,de->rje", normed, w_gate, preferred_element_type=jnp.float32)
    )
    update = (gate * linear).astype(jnp.bfloat16).reshape(rows, 1, cols, width)
    return lax.all_to_all(update, "blk", split_axis=2, concat_axis=0, tiled=True)


MESH = pl.DeviceIdType.MESH
CELLS = 16
GROUP = 8
PIECE = 4


def dot(a, b, contract):
    return lax.dot_general(a, b, ((contract[:1], contract[1:]), ((), ())), preferred_element_type=jnp.float32)


def kernel(blocks, chans, halves, *refs):
    sources, out, targets = refs[:9], refs[9], refs[10:19]
    fetched = refs[19]
    (
        swap, normed, cells, pick, sides, sides_in, tri_f, tri, tri_in, squares, rows_out,
        side_send, side_recv, cell_send, cell_recv, tri_send, tri_recv,
    ) = refs[20:]
    act, mask, in_gain, in_bias, w_proj, w_gate, w_out, out_gain, out_bias = targets
    fetches = [
        pltpu.make_async_copy(source, target, fetched.at[n])
        for n, (source, target) in enumerate(zip(sources, targets))
    ]
    for fetch in fetches:
        fetch.start()
    slabs = chans * halves
    devices = blocks * slabs
    blk = lax.axis_index("blk")
    chan = lax.axis_index("chan")
    half = lax.axis_index("pair")
    slab = chan * halves + half
    me = slab * blocks + blk
    blks = (blk, blk + 1 - 2 * (blk % 2), (blk + 2) % 4, 3 - blk)
    chan_of = (chan, 1 - chan)
    half_of = (half, 1 - half)

    def peer(n):
        b, c, p = blks[n // 4], chan_of[n // 2 % 2], half_of[n % 2]
        s = c * halves + p
        return s, b, s * blocks + b, {"blk": b, "chan": c, "pair": p}

    barrier = pltpu.get_barrier_semaphore()
    for n in range(1, devices):
        pl.semaphore_signal(barrier, inc=1, device_id=peer(n)[3], device_id_type=MESH)

    lanes = CELLS * CELLS
    row = lax.broadcasted_iota(jnp.int32, (CELLS, lanes), 0)
    lane = lax.broadcasted_iota(jnp.int32, (CELLS, lanes), 1)
    spread = jnp.where(lane // CELLS == row, 1.0, 0.0).astype(jnp.bfloat16)
    own_row = lane % CELLS == row
    total = slabs * CELLS
    at = lax.broadcasted_iota(jnp.int32, (lanes, total), 0)
    col = lax.broadcasted_iota(jnp.int32, (lanes, total), 1)
    for s in range(slabs):
        pick[s] = jnp.where(col == at // CELLS + s * CELLS, 1.0, 0.0).astype(jnp.bfloat16)
    moved = (row % GROUP) // 2 * PIECE + row // GROUP * 2 + row % 2
    right_row = lane % CELLS == moved
    for fetch in fetches[:4]:
        fetch.wait()

    x = act[...].astype(jnp.float32)
    mean = jnp.mean(x, axis=-1, keepdims=True)
    centred = x - mean
    var = jnp.mean(centred * centred, axis=-1, keepdims=True)
    x = centred * lax.rsqrt(var + 1e-05) * in_gain[...].reshape(1, 1, -1) + in_bias[...].reshape(1, 1, -1)
    for i in range(CELLS):
        swap[pl.ds(i, CELLS, stride=CELLS), :] = x[i]
    z = swap[...].astype(jnp.bfloat16)
    normed[...] = z.reshape(normed.shape)

    mask_rows = dot(mask[...].astype(jnp.float32).astype(jnp.bfloat16), spread, (1, 0))
    mask_row = jnp.sum(jnp.where(own_row, mask_rows, 0.0), axis=0, keepdims=True)

    fetches[4].wait()
    proj = dot(w_proj[...], z, (0, 1))
    hidden = proj.shape[0] // 4
    left = jax.nn.sigmoid(proj[:hidden]) * proj[hidden:2 * hidden] * mask_row
    right = jax.nn.sigmoid(proj[2 * hidden:3 * hidden]) * proj[3 * hidden:] * mask_row
    groups = hidden // GROUP
    both = jnp.concatenate(
        [left.reshape(groups, GROUP, lanes), right.reshape(groups, GROUP, lanes)], axis=1
    )
    sides[...] = both.astype(jnp.bfloat16)

    pl.semaphore_wait(barrier, devices - 1)
    copies = []
    for n in range(devices - 1, 0, -1):
        _, _, to, device = peer(n)
        copy = pltpu.make_async_remote_copy(
            src_ref=sides.at[to], dst_ref=sides_in.at[n],
            send_sem=side_send.at[n], recv_sem=side_recv.at[n],
            device_id=device, device_id_type=MESH,
        )
        copy.start()
        copies.append(copy)
    sides_in[0] = sides[me]
    cells[blk] = normed[pl.ds(blk * PIECE, PIECE)]

    for fetch in fetches[5:]:
        fetch.wait()
    gain = jnp.transpose(jnp.broadcast_to(out_gain[...].reshape(1, -1), (hidden, hidden))).reshape(groups, GROUP, hidden)
    bias = jnp.transpose(jnp.broadcast_to(out_bias[...].reshape(1, -1), (hidden, hidden))).reshape(groups, GROUP, hidden)

    def send_cells():
        for n in range(1, blocks):
            b = blks[n]
            copy = pltpu.make_async_remote_copy(
                src_ref=normed.at[pl.ds(b * PIECE, PIECE)], dst_ref=cells.at[blk],
                send_sem=cell_send.at[n], recv_sem=cell_recv.at[n],
                device_id={"blk": b}, device_id_type=MESH,
            )
            copy.start()
            copies.append(copy)

    for nb in (0, 1, 3, 2):
        if nb == 2:
            send_cells()
        acc = None
        for n in range(nb * slabs, nb * slabs + slabs):
            s, b, frm, device = peer(n)
            if n:
                pltpu.make_async_remote_copy(
                    src_ref=sides.at[frm], dst_ref=sides_in.at[n],
                    send_sem=side_send.at[n], recv_sem=side_recv.at[n],
                    device_id=device, device_id_type=MESH,
                ).wait_recv()
            part = sides_in[n].astype(jnp.float32)
            part_left = jnp.where(own_row[None], part[:GROUP][:, None, :], 0.0)
            part_right = jnp.where(right_row[None], part[GROUP:][:, None, :], 0.0)
            wide = jnp.concatenate([part_left, part_right], axis=0).reshape(2 * GROUP * CELLS, lanes)
            term = dot(wide.astype(jnp.bfloat16), pick[s], (1, 0))
            acc = term if acc is None else acc + term
        rows_of = pl.ds(pl.multiple_of(b * CELLS, CELLS), CELLS)
        block = acc.astype(jnp.bfloat16).reshape(2 * GROUP, CELLS, total)
        squares[:, rows_of, :] = block

    wide_rows = blocks * GROUP
    for h in range(GROUP):
        t = dot(squares[GROUP + h], squares[h], (1, 1)).reshape(blocks, 2, GROUP, total)
        t = jnp.concatenate([t[:, 0], t[:, 1]], axis=-1).reshape(wide_rows, 2 * total)
        tri_f[pl.ds(h, wide_rows, stride=GROUP), :] = t
    tri[...] = tri_f[...].astype(jnp.bfloat16).reshape(tri.shape)

    for n in range(devices - 1, 0, -1):
        _, _, to, device = peer(n)
        copy = pltpu.make_async_remote_copy(
            src_ref=tri.at[to], dst_ref=tri_in.at[me],
            send_sem=tri_send.at[n], recv_sem=tri_recv.at[n],
            device_id=device, device_id_type=MESH,
        )
        copy.start()
        copies.append(copy)
    tri_in[me] = tri[me]
    for copy in copies[:1 - devices]:
        copy.wait_send()

    for n in range(1, blocks):
        b = blks[n]
        pltpu.make_async_remote_copy(
            src_ref=cells.at[b], dst_ref=cells.at[b],
            send_sem=cell_send.at[n], recv_sem=cell_recv.at[n],
            device_id={"blk": b}, device_id_type=MESH,
        ).wait_recv()
    mine = jnp.concatenate([cells[b, m] for m in range(PIECE) for b in range(blocks)], axis=0)
    gate = jax.nn.sigmoid(dot(mine, w_gate[...], (1, 0)))
    for copy in copies[1 - devices:]:
        copy.wait_send()

    for n in range(1, devices):
        _, _, frm, device = peer(n)
        pltpu.make_async_remote_copy(
            src_ref=tri.at[frm], dst_ref=tri_in.at[frm],
            send_sem=tri_send.at[n], recv_sem=tri_recv.at[n],
            device_id=device, device_id_type=MESH,
        ).wait_recv()
    full = tri_in[...].astype(jnp.float32).reshape(groups, 2, GROUP, hidden)
    for q in range(2):
        t = full[:, q]
        mean = jnp.mean(t, axis=(0, 1), keepdims=True)
        centred = t - mean
        var = jnp.mean(centred * centred, axis=(0, 1), keepdims=True)
        t = centred * lax.rsqrt(var + 1e-05) * gain + bias
        linear = dot(t.reshape(hidden, hidden).astype(jnp.bfloat16), w_out[...], (0, 0))
        for p in range(2):
            m = p * 2 + q
            rows_out[pl.ds(m, total, stride=PIECE), :] = linear[p * total:(p + 1) * total] * gate[m * total:(m + 1) * total]
    out[...] = rows_out[...].astype(jnp.bfloat16)


def in_one_kernel(*args):
    blocks = lax.axis_size("blk")
    chans = lax.axis_size("chan")
    halves = lax.axis_size("pair")
    rows, cols, width = args[0].shape
    slabs = chans * halves
    devices = blocks * slabs
    total = rows * blocks
    bf16, f32 = jnp.bfloat16, jnp.float32
    dma = pltpu.SemaphoreType.DMA
    vmem = pl.BlockSpec(memory_space=pltpu.VMEM)
    out = pl.pallas_call(
        functools.partial(kernel, blocks, chans, halves),
        out_shape=pltpu.VMEM((total * PIECE, width), bf16),
        in_specs=[pl.BlockSpec(memory_space=pltpu.HBM)] * len(args),
        out_specs=vmem,
        scratch_shapes=[pltpu.VMEM(a.shape, a.dtype) for a in args] + [
            dma((len(args),)),
            pltpu.VMEM((rows * cols, width), f32),
            pltpu.VMEM((cols, rows, width), bf16),
            pltpu.VMEM((blocks, PIECE, rows, width), bf16),
            pltpu.VMEM((slabs, rows * cols, total), bf16),
            pltpu.VMEM((devices, 2 * GROUP, rows * cols), bf16),
            pltpu.VMEM((devices, 2 * GROUP, rows * cols), bf16),
            pltpu.VMEM((devices * 2 * GROUP, 2 * total), f32),
            pltpu.VMEM((devices, 2 * GROUP, 2 * total), bf16),
            pltpu.VMEM((devices, 2 * GROUP, 2 * total), bf16),
            pltpu.VMEM((2 * GROUP, total, total), bf16),
            pltpu.VMEM((total * PIECE, width), f32),
            dma((devices,)),
            dma((devices,)),
            dma((blocks,)),
            dma((blocks,)),
            dma((devices,)),
            dma((devices,)),
        ],
        compiler_params=pltpu.CompilerParams(
            collective_id=0, has_side_effects=True, vmem_limit_bytes=60 * 2**20
        ),
    )(*args)
    return out.reshape(total, 1, PIECE, width)


def fits(mesh, act_shape, hidden):
    groups, blocks, chans, halves = (mesh.shape[a] for a in ("groups", "blk", "chan", "pair"))
    slabs = chans * halves
    rows, cols = act_shape[0] // (groups * blocks), act_shape[1] // slabs
    return (
        (rows, cols) == (CELLS, CELLS)
        and act_shape[2] == hidden == 128
        and blocks * slabs * GROUP == hidden
        and (blocks, chans, halves) == (4, 2, 2)
    )


def solution(mesh):
    specs = (P(("groups", "blk"), ("chan", "pair"), None), P(("groups", "blk"), ("chan", "pair"))) + (P(),) * 7

    def run(*args):
        body = in_one_kernel if fits(mesh, args[0].shape, args[6].shape[0]) else on_device
        return jax.shard_map(
            body,
            mesh=mesh,
            in_specs=specs,
            out_specs=P("groups", ("chan", "pair"), "blk", None),
            check_vma=False,
        )(*args)

    return run
```

```python
import functools

import jax
import jax.numpy as jnp
from jax import lax
from jax.experimental import pallas as pl
from jax.experimental.pallas import tpu as pltpu
from jax.sharding import PartitionSpec as P


def from_behind(value, axis, by):
    count = lax.axis_size(axis)
    return lax.ppermute(value, axis, [(i, (i + by) % count) for i in range(count)])


def norm_axis(values, gain, bias, axis):
    mean = jnp.mean(values, axis=axis, keepdims=True)
    centred = values - mean
    var = jnp.mean(centred * centred, axis=axis, keepdims=True)
    return centred * lax.rsqrt(var + 1e-05) * gain + bias


def on_device(pair_act, pair_mask, in_gain, in_bias, w_proj, w_gate, w_out, out_gain, out_bias):
    rows, cols, width = pair_act.shape
    hidden = w_out.shape[0]
    blocks = lax.axis_size("blk")
    chans = lax.axis_size("chan")
    halves = lax.axis_size("pair")
    normed = norm_axis(pair_act.astype(jnp.float32), in_gain, in_bias, -1).astype(jnp.bfloat16)
    weights = w_proj.reshape(width, 4, hidden)
    proj = jnp.einsum("rkd,dgh->ghrk", normed, weights, preferred_element_type=jnp.float32)
    mask_f = pair_mask.astype(jnp.float32)
    left = (jax.nn.sigmoid(proj[0]) * proj[1] * mask_f).astype(jnp.bfloat16)
    right = (jax.nn.sigmoid(proj[2]) * proj[3] * mask_f).astype(jnp.bfloat16)
    left, right = (
        lax.all_to_all(left, "chan", split_axis=0, concat_axis=2, tiled=True),
        lax.all_to_all(right, "chan", split_axis=0, concat_axis=2, tiled=True),
    )
    subset = left.shape[0]
    me_index = lax.axis_index("blk")
    total = rows * blocks
    zero_index = jnp.zeros((), jnp.int32)

    def place(acc, block, owner):
        part = jnp.einsum("cik,cjk->cij", left, block, preferred_element_type=jnp.float32)
        start = owner * rows
        return lax.dynamic_update_slice(acc, part, (zero_index, zero_index, start))

    acc = jnp.zeros((subset, rows, total), jnp.float32)
    acc = place(acc, right, me_index)

    def both_step(step, carry):
        acc_now, ahead, behind = carry
        ahead = from_behind(ahead, "blk", 1)
        behind = from_behind(behind, "blk", -1)
        acc_now = place(acc_now, ahead, (me_index - step) % blocks)
        acc_now = place(acc_now, behind, (me_index + step) % blocks)
        return (acc_now, ahead, behind)

    acc, ahead, behind = lax.fori_loop(1, (blocks - 1) // 2 + 1, both_step, (acc, right, right))
    ahead = from_behind(ahead, "blk", 1)
    acc = place(acc, ahead, (me_index - blocks // 2) % blocks)
    parts = acc.reshape(subset, rows, chans, halves, cols)
    mine = lax.psum_scatter(parts, "pair", scatter_dimension=3, tiled=True)
    full = lax.all_to_all(mine, "chan", split_axis=2, concat_axis=0, tiled=True)
    full = full.reshape(hidden, rows, cols)
    tri_norm = norm_axis(full, out_gain[:, None, None], out_bias[:, None, None], 0).astype(
        jnp.bfloat16
    )
    linear = jnp.einsum("hrj,hd->rjd", tri_norm, w_out, preferred_element_type=jnp.float32)
    gate = jax.nn.sigmoid(
        jnp.einsum("rjd,de->rje", normed, w_gate, preferred_element_type=jnp.float32)
    )
    update = (gate * linear).astype(jnp.bfloat16).reshape(rows, 1, cols, width)
    return lax.all_to_all(update, "blk", split_axis=2, concat_axis=0, tiled=True)


MESH = pl.DeviceIdType.MESH
CELLS = 16
GROUP = 8
PIECE = 4


def dot(a, b, contract):
    return lax.dot_general(a, b, ((contract[:1], contract[1:]), ((), ())), preferred_element_type=jnp.float32)


def kernel(blocks, chans, halves, *refs):
    sources, out, targets = refs[:9], refs[9], refs[10:19]
    fetched = refs[19]
    (
        swap, normed, cells, pick, sides, sides_in, tri_f, tri, tri_in, squares, rows_out,
        side_send, side_recv, cell_send, cell_recv, tri_send, tri_recv,
    ) = refs[20:]
    act, mask, in_gain, in_bias, w_proj, w_gate, w_out, out_gain, out_bias = targets
    fetches = [
        pltpu.make_async_copy(source, target, fetched.at[n])
        for n, (source, target) in enumerate(zip(sources, targets))
    ]
    for fetch in fetches:
        fetch.start()
    slabs = chans * halves
    devices = blocks * slabs
    blk = lax.axis_index("blk")
    chan = lax.axis_index("chan")
    half = lax.axis_index("pair")
    slab = chan * halves + half
    me = slab * blocks + blk
    blks = (blk, blk + 1 - 2 * (blk % 2), (blk + 2) % 4, 3 - blk)
    chan_of = (chan, 1 - chan)
    half_of = (half, 1 - half)

    def peer(n):
        b, c, p = blks[n // 4], chan_of[n // 2 % 2], half_of[n % 2]
        s = c * halves + p
        return s, b, s * blocks + b, {"blk": b, "chan": c, "pair": p}

    barrier = pltpu.get_barrier_semaphore()
    for n in range(1, devices):
        pl.semaphore_signal(barrier, inc=1, device_id=peer(n)[3], device_id_type=MESH)

    lanes = CELLS * CELLS
    row = lax.broadcasted_iota(jnp.int32, (CELLS, lanes), 0)
    lane = lax.broadcasted_iota(jnp.int32, (CELLS, lanes), 1)
    spread = jnp.where(lane // CELLS == row, 1.0, 0.0).astype(jnp.bfloat16)
    own_row = lane % CELLS == row
    total = slabs * CELLS
    at = lax.broadcasted_iota(jnp.int32, (lanes, total), 0)
    col = lax.broadcasted_iota(jnp.int32, (lanes, total), 1)
    for s in range(slabs):
        pick[s] = jnp.where(col == at // CELLS + s * CELLS, 1.0, 0.0).astype(jnp.bfloat16)
    moved = (row % GROUP) // 2 * PIECE + row // GROUP * 2 + row % 2
    right_row = lane % CELLS == moved
    for fetch in fetches[:4]:
        fetch.wait()

    x = act[...].astype(jnp.float32)
    mean = jnp.mean(x, axis=-1, keepdims=True)
    centred = x - mean
    var = jnp.mean(centred * centred, axis=-1, keepdims=True)
    x = centred * lax.rsqrt(var + 1e-05) * in_gain[...].reshape(1, 1, -1) + in_bias[...].reshape(1, 1, -1)
    for i in range(CELLS):
        swap[pl.ds(i, CELLS, stride=CELLS), :] = x[i]
    z = swap[...].astype(jnp.bfloat16)
    normed[...] = z.reshape(normed.shape)

    mask_rows = dot(mask[...].astype(jnp.float32).astype(jnp.bfloat16), spread, (1, 0))
    mask_row = jnp.sum(jnp.where(own_row, mask_rows, 0.0), axis=0, keepdims=True)

    fetches[4].wait()
    proj = dot(w_proj[...], z, (0, 1))
    hidden = proj.shape[0] // 4
    left = jax.nn.sigmoid(proj[:hidden]) * proj[hidden:2 * hidden] * mask_row
    right = jax.nn.sigmoid(proj[2 * hidden:3 * hidden]) * proj[3 * hidden:] * mask_row
    groups = hidden // GROUP
    both = jnp.concatenate(
        [left.reshape(groups, GROUP, lanes), right.reshape(groups, GROUP, lanes)], axis=1
    )
    sides[...] = both.astype(jnp.bfloat16)

    pl.semaphore_wait(barrier, devices - 1)
    copies = []
    for n in range(devices - 1, 0, -1):
        _, _, to, device = peer(n)
        copy = pltpu.make_async_remote_copy(
            src_ref=sides.at[to], dst_ref=sides_in.at[n],
            send_sem=side_send.at[n], recv_sem=side_recv.at[n],
            device_id=device, device_id_type=MESH,
        )
        copy.start()
        copies.append(copy)
    sides_in[0] = sides[me]
    cells[blk] = normed[pl.ds(blk * PIECE, PIECE)]

    for fetch in fetches[5:]:
        fetch.wait()
    gain = jnp.transpose(jnp.broadcast_to(out_gain[...].reshape(1, -1), (hidden, hidden))).reshape(groups, GROUP, hidden)
    bias = jnp.transpose(jnp.broadcast_to(out_bias[...].reshape(1, -1), (hidden, hidden))).reshape(groups, GROUP, hidden)

    def send_cells():
        for n in range(1, blocks):
            b = blks[n]
            copy = pltpu.make_async_remote_copy(
                src_ref=normed.at[pl.ds(b * PIECE, PIECE)], dst_ref=cells.at[blk],
                send_sem=cell_send.at[n], recv_sem=cell_recv.at[n],
                device_id={"blk": b}, device_id_type=MESH,
            )
            copy.start()
            copies.append(copy)

    for nb in (0, 1, 3, 2):
        if nb == 3:
            send_cells()
        acc = None
        for n in range(nb * slabs, nb * slabs + slabs):
            s, b, frm, device = peer(n)
            if n:
                pltpu.make_async_remote_copy(
                    src_ref=sides.at[frm], dst_ref=sides_in.at[n],
                    send_sem=side_send.at[n], recv_sem=side_recv.at[n],
                    device_id=device, device_id_type=MESH,
                ).wait_recv()
            part = sides_in[n].astype(jnp.float32)
            part_left = jnp.where(own_row[None], part[:GROUP][:, None, :], 0.0)
            part_right = jnp.where(right_row[None], part[GROUP:][:, None, :], 0.0)
            wide = jnp.concatenate([part_left, part_right], axis=0).reshape(2 * GROUP * CELLS, lanes)
            term = dot(wide.astype(jnp.bfloat16), pick[s], (1, 0))
            acc = term if acc is None else acc + term
        rows_of = pl.ds(pl.multiple_of(b * CELLS, CELLS), CELLS)
        block = acc.astype(jnp.bfloat16).reshape(2 * GROUP, CELLS, total)
        squares[:, rows_of, :] = block

    wide_rows = blocks * GROUP
    for h in range(GROUP):
        t = dot(squares[GROUP + h], squares[h], (1, 1)).reshape(blocks, 2, GROUP, total)
        t = jnp.concatenate([t[:, 0], t[:, 1]], axis=-1).reshape(wide_rows, 2 * total)
        tri_f[pl.ds(h, wide_rows, stride=GROUP), :] = t
    tri[...] = tri_f[...].astype(jnp.bfloat16).reshape(tri.shape)

    for n in range(devices - 1, 0, -1):
        _, _, to, device = peer(n)
        copy = pltpu.make_async_remote_copy(
            src_ref=tri.at[to], dst_ref=tri_in.at[me],
            send_sem=tri_send.at[n], recv_sem=tri_recv.at[n],
            device_id=device, device_id_type=MESH,
        )
        copy.start()
        copies.append(copy)
    tri_in[me] = tri[me]
    for copy in copies[:1 - devices]:
        copy.wait_send()

    for n in range(1, blocks):
        b = blks[n]
        pltpu.make_async_remote_copy(
            src_ref=cells.at[b], dst_ref=cells.at[b],
            send_sem=cell_send.at[n], recv_sem=cell_recv.at[n],
            device_id={"blk": b}, device_id_type=MESH,
        ).wait_recv()
    mine = jnp.concatenate([cells[b, m] for m in range(PIECE) for b in range(blocks)], axis=0)
    gate = jax.nn.sigmoid(dot(mine, w_gate[...], (1, 0)))
    for copy in copies[1 - devices:]:
        copy.wait_send()

    for n in range(1, devices):
        _, _, frm, device = peer(n)
        pltpu.make_async_remote_copy(
            src_ref=tri.at[frm], dst_ref=tri_in.at[frm],
            send_sem=tri_send.at[n], recv_sem=tri_recv.at[n],
            device_id=device, device_id_type=MESH,
        ).wait_recv()
    full = tri_in[...].astype(jnp.float32).reshape(groups, 2, GROUP, hidden)
    for q in range(2):
        t = full[:, q]
        mean = jnp.mean(t, axis=(0, 1), keepdims=True)
        centred = t - mean
        var = jnp.mean(centred * centred, axis=(0, 1), keepdims=True)
        t = centred * lax.rsqrt(var + 1e-05) * gain + bias
        linear = dot(t.reshape(hidden, hidden).astype(jnp.bfloat16), w_out[...], (0, 0))
        for p in range(2):
            m = p * 2 + q
            rows_out[pl.ds(m, total, stride=PIECE), :] = linear[p * total:(p + 1) * total] * gate[m * total:(m + 1) * total]
    out[...] = rows_out[...].astype(jnp.bfloat16)


def in_one_kernel(*args):
    blocks = lax.axis_size("blk")
    chans = lax.axis_size("chan")
    halves = lax.axis_size("pair")
    rows, cols, width = args[0].shape
    slabs = chans * halves
    devices = blocks * slabs
    total = rows * blocks
    bf16, f32 = jnp.bfloat16, jnp.float32
    dma = pltpu.SemaphoreType.DMA
    vmem = pl.BlockSpec(memory_space=pltpu.VMEM)
    out = pl.pallas_call(
        functools.partial(kernel, blocks, chans, halves),
        out_shape=pltpu.VMEM((total * PIECE, width), bf16),
        in_specs=[pl.BlockSpec(memory_space=pltpu.HBM)] * len(args),
        out_specs=vmem,
        scratch_shapes=[pltpu.VMEM(a.shape, a.dtype) for a in args] + [
            dma((len(args),)),
            pltpu.VMEM((rows * cols, width), f32),
            pltpu.VMEM((cols, rows, width), bf16),
            pltpu.VMEM((blocks, PIECE, rows, width), bf16),
            pltpu.VMEM((slabs, rows * cols, total), bf16),
            pltpu.VMEM((devices, 2 * GROUP, rows * cols), bf16),
            pltpu.VMEM((devices, 2 * GROUP, rows * cols), bf16),
            pltpu.VMEM((devices * 2 * GROUP, 2 * total), f32),
            pltpu.VMEM((devices, 2 * GROUP, 2 * total), bf16),
            pltpu.VMEM((devices, 2 * GROUP, 2 * total), bf16),
            pltpu.VMEM((2 * GROUP, total, total), bf16),
            pltpu.VMEM((total * PIECE, width), f32),
            dma((devices,)),
            dma((devices,)),
            dma((blocks,)),
            dma((blocks,)),
            dma((devices,)),
            dma((devices,)),
        ],
        compiler_params=pltpu.CompilerParams(
            collective_id=0, has_side_effects=True, vmem_limit_bytes=60 * 2**20
        ),
    )(*args)
    return out.reshape(total, 1, PIECE, width)


def fits(mesh, act_shape, hidden):
    groups, blocks, chans, halves = (mesh.shape[a] for a in ("groups", "blk", "chan", "pair"))
    slabs = chans * halves
    rows, cols = act_shape[0] // (groups * blocks), act_shape[1] // slabs
    return (
        (rows, cols) == (CELLS, CELLS)
        and act_shape[2] == hidden == 128
        and blocks * slabs * GROUP == hidden
        and (blocks, chans, halves) == (4, 2, 2)
    )


def solution(mesh):
    specs = (P(("groups", "blk"), ("chan", "pair"), None), P(("groups", "blk"), ("chan", "pair"))) + (P(),) * 7

    def run(*args):
        body = in_one_kernel if fits(mesh, args[0].shape, args[6].shape[0]) else on_device
        return jax.shard_map(
            body,
            mesh=mesh,
            in_specs=specs,
            out_specs=P("groups", ("chan", "pair"), "blk", None),
            check_vma=False,
        )(*args)

    return run
```
